32 devices in a mesh: grp: 2 (over x), ch: 4 (over y, core), sp: 4 (over z).
Axes of the slice: x: 2, y: 2, z: 4, core: 2. Of those that a mesh axis runs over, the one named last changes fastest.
Arguments:
- features: bfloat16 [1024, 64, 128], P(('grp', 'ch'), 'sp'), parts along dimension 0, may hold values from -6 to 6
- saved_mix: bfloat16 [1024, 64, 128], P(('grp', 'ch'), 'sp'), parts along dimension 0, may hold values from -6 to 6
- out_grad: bfloat16 [1024, 64, 128], P(('grp', 'ch'), 'sp'), parts along dimension 0, may hold values from -6 to 6
- kernel: bfloat16 [512, 31, 31], P('ch'), may hold values from -0.1875 to 0.1875
- w_in: bfloat16 [512, 2048], P(None, 'ch'), may hold values from -0.25 to 0.25
- w_out: bfloat16 [2048, 512], P('ch'), may hold values from -0.125 to 0.125
Outputs:
- in_grad: float32 [1024, 64, 128], P(('grp', 'ch'), 'sp'), parts along dimension 0
- kernel_grad: float32 [1024, 31, 31], P(('grp', 'ch')), parts along dimension 0
- w_in_grad: float32 [1024, 2048], P('grp', ('ch', 'sp')), parts along dimension 0
- w_out_grad: float32 [4096, 512], P(('grp', 'ch', 'sp')), parts along dimension 0
The draws below stay inside these ranges and needn't reach their ends.
There are 2 independent parts, one for each index of `grp`. The reference program is written for one: setup_inputs(seed, part) draws one part's arguments, and reference() takes and returns one part's arrays. A program takes and returns all parts, laid end to end along the dimension named above; an argument that names none is the same for every part. Nothing has to cross between parts.
All inputs are finite; a program needn't handle non-finite values.
Results may differ from the reference program's by a relative error of at most 0.0041.
Values may be sent and summed in bfloat16 or wider, within the bound.
A program may use at most 64 MiB of HBM per device.

```python
import math
import jax
import jax.numpy as jnp
from jax import lax

C = 512
FF = 2048
KS = 31
COLS = 128
ROWS = 64


def steps_of(stream_key, shape, shards, least, largest):
    level = 1.0
    for position, shards_of in shards:
        steps = jax.random.uniform(jax.random.fold_in(jax.random.fold_in(stream_key, 6), position), (shards_of,), jnp.float32, least / len(shards), largest / len(shards))
        level = level * jnp.repeat(jnp.exp(steps), shape[position] // shards_of).reshape((-1,) + (1,) * (len(shape) - 1 - position))
    return level


def bell_draw(key, dims, scale, limit, pieces=(), dtype=jnp.bfloat16):
    level = steps_of(key, dims, pieces, -0.22, 0.18) if pieces else 1.0
    entries = jax.random.normal(key, dims, jnp.float32) * scale * level
    return jnp.minimum(jnp.maximum(entries, -limit), limit).astype(dtype)


def setup_inputs(seed: int = 0, part: int = 0) -> dict:
    arg_keys = jax.random.split(jax.random.key(seed), 7)
    own_keys = jax.random.split(jax.random.fold_in(arg_keys[6], part), 7)
    return {
        "features": bell_draw(own_keys[0], (C, ROWS, COLS), 1.0, 6.0, ((0, 4), (1, 4))),
        "saved_mix": bell_draw(own_keys[1], (C, ROWS, COLS), 1.0, 6.0, ((0, 4), (1, 4))),
        "out_grad": bell_draw(own_keys[2], (C, ROWS, COLS), 1.0, 6.0, ((0, 4), (1, 4))),
        "kernel": bell_draw(arg_keys[3], (C, KS, KS), (KS * KS) ** -0.5, 0.1875, ((0, 4),)),
        "w_in": bell_draw(arg_keys[4], (C, FF), C ** -0.5, 0.25, ((1, 4),)),
        "w_out": bell_draw(arg_keys[5], (FF, C), FF ** -0.5, 0.125, ((0, 4),)),
    }


SQRT_HALF = 0.7071067811865476
INV_ROOT_TAU = 0.3989422804014327

def depthwise(source, taps):
    return lax.conv_general_dilated(source[None], taps[:, None], (1, 1), 'VALID', dimension_numbers=('NCHW', 'OIHW', 'NCHW'), feature_group_count=source.shape[0], preferred_element_type=jnp.float32)[0]

def blocked_depthwise(source, taps):
    channels = source.shape[0]
    group = math.gcd(channels, 16)
    count = channels // group
    source_blocks = source.reshape((count, group) + source.shape[1:])
    tap_blocks = taps.reshape((count, group) + taps.shape[1:])
    result = lax.map(lambda pair: depthwise(pair[0], pair[1]), (source_blocks, tap_blocks))
    return result.reshape((channels,) + result.shape[2:])

def contract_last(left, right):
    return lax.dot_general(left, right, (((1,), (1,)), ((), ())), preferred_element_type=jnp.float32)

def contract_first(left, right):
    return lax.dot_general(left, right, (((0,), (0,)), ((), ())), preferred_element_type=jnp.float32)

def reference(features, saved_mix, out_grad, kernel, w_in, w_out):
    channels, height, width = features.shape
    positions = height * width
    hidden_units = w_in.shape[1]
    half = kernel.shape[1] // 2
    factor = 1.0 / math.sqrt(positions)
    block = math.gcd(positions, 1024)
    count = positions // block
    mixed_blocks = saved_mix.reshape(channels, count, block).transpose(1, 0, 2)
    grad_blocks = out_grad.reshape(channels, count, block).transpose(1, 0, 2)

    def step_block(carry, pair):
        in_acc, out_acc = carry
        mixed_rows, grad_rows = pair
        preact = contract_first(w_in, mixed_rows)
        normal_cdf = 0.5 * (1.0 + jax.scipy.special.erf(preact * SQRT_HALF))
        normal_pdf = INV_ROOT_TAU * jnp.exp(-0.5 * preact * preact)
        hidden = (preact * normal_cdf).astype(jnp.bfloat16)
        hidden_grad = jnp.dot(w_out, grad_rows, preferred_element_type=jnp.float32)
        preact_grad = (hidden_grad * (normal_cdf + preact * normal_pdf)).astype(jnp.bfloat16)
        in_acc = in_acc + contract_last(mixed_rows, preact_grad)
        out_acc = out_acc + contract_last(hidden, grad_rows)
        mix_block = jnp.dot(w_in, preact_grad, preferred_element_type=jnp.float32).astype(jnp.bfloat16)
        return ((in_acc, out_acc), mix_block)
    start = (jnp.zeros((channels, hidden_units), jnp.float32), jnp.zeros((hidden_units, channels), jnp.float32))
    (in_acc, out_acc), mix_blocks = lax.scan(step_block, start, (mixed_blocks, grad_blocks))
    w_in_grad = in_acc * factor
    w_out_grad = out_acc * factor
    mix_grad = mix_blocks.transpose(1, 0, 2).reshape(channels, height, width)
    padded = jnp.pad(mix_grad, ((0, 0), (half, half), (half, half)))
    in_grad = out_grad.astype(jnp.float32) + blocked_depthwise(padded, kernel[:, ::-1, ::-1])
    kernel_grad = blocked_depthwise(padded, features)[:, ::-1, ::-1] * factor
    return (in_grad, kernel_grad, w_in_grad, w_out_grad)
```

```python
import functools
import math

import jax
import jax.numpy as jnp
from jax import lax
from jax.experimental import pallas as pl
from jax.experimental.pallas import tpu as pltpu
from jax.sharding import PartitionSpec as P

SQRT_HALF = 0.7071067811865476
INV_ROOT_TAU = 0.3989422804014327
GROUP = 8


def up(count, unit):
    return -(-count // unit) * unit


def conv_kernel(size, rim_ref, feat_ref, grad_ref, base_ref, in_ref, part_ref):
    group, depth, width = rim_ref.shape
    rows = feat_ref.shape[1]
    half = size // 2
    total = base_ref.shape[1]
    lane = lax.broadcasted_iota(jnp.int32, (depth, width), 1)
    for c in range(group):
        rim = rim_ref[c]
        pieces = []
        for b in range(size):
            shift = b - half
            if shift == 0:
                pieces.append(rim)
                continue
            moved = pltpu.roll(rim, (-shift) % width, 1)
            inside = (lane < width - shift) if shift > 0 else (lane >= -shift)
            pieces.append(jnp.where(inside, moved, jnp.zeros_like(moved)))
        pieces.append(jnp.zeros((total - size * depth, width), rim.dtype))
        stacked = jnp.concatenate(pieces, axis=0)
        line = jnp.broadcast_to(base_ref[c : c + 1, :], (rows, total))
        band = pltpu.roll(line, 0, 1, stride=1, stride_axis=0).astype(jnp.bfloat16)
        in_ref[c] = grad_ref[c].astype(jnp.float32) + jnp.dot(
            band, stacked, preferred_element_type=jnp.float32
        )
        cross = lax.dot_general(
            feat_ref[c], stacked, (((1,), (1,)), ((), ())), preferred_element_type=jnp.float32
        )
        aligned = pltpu.roll(cross, total - (rows - 1), 1, stride=1, stride_axis=0)
        part_ref[c : c + 1, :] = jnp.sum(aligned, axis=0, keepdims=True)


def conv_back(rim, feat_reversed, grad, base, size):
    channels, depth, width = rim.shape
    rows = feat_reversed.shape[1]
    total = base.shape[1]
    group = math.gcd(channels, GROUP)
    block = lambda *dims: pl.BlockSpec((group,) + dims, lambda i: (i,) + (0,) * len(dims))
    return pl.pallas_call(
        functools.partial(conv_kernel, size),
        grid=(channels // group,),
        out_shape=(
            jax.ShapeDtypeStruct((channels, rows, width), jnp.float32),
            jax.ShapeDtypeStruct((channels, total), jnp.float32),
        ),
        in_specs=[block(depth, width), block(rows, width), block(rows, width), block(total)],
        out_specs=(block(rows, width), block(total)),
        compiler_params=pltpu.CompilerParams(vmem_limit_bytes=24 * 1024 * 1024),
        cost_estimate=pl.CostEstimate(
            flops=channels * rows * width * total * 4 * 8,
            bytes_accessed=channels * width * (depth * 2 + rows * 8) + channels * total * 8,
            transcendentals=0,
        ),
    )(rim, feat_reversed, grad, base)


def contract_last(left, right):
    return lax.dot_general(
        left, right, (((1,), (1,)), ((), ())), preferred_element_type=jnp.float32
    )


def contract_first(left, right):
    return lax.dot_general(
        left, right, (((0,), (0,)), ((), ())), preferred_element_type=jnp.float32
    )


def matmul(left, right):
    return jnp.dot(left, right, preferred_element_type=jnp.float32)


def pointwise_back(mixed_rows, grad_rows, w_in_block, w_out_block):
    preact = contract_first(w_in_block, mixed_rows)
    normal_cdf = 0.5 * (1.0 + jax.scipy.special.erf(preact * SQRT_HALF))
    normal_pdf = INV_ROOT_TAU * jnp.exp(-0.5 * preact * preact)
    hidden = (preact * normal_cdf).astype(jnp.bfloat16)
    hidden_grad = matmul(w_out_block, grad_rows)
    preact_grad = (hidden_grad * (normal_cdf + preact * normal_pdf)).astype(jnp.bfloat16)
    return (hidden, preact_grad)


def per_device(features, saved_mix, out_grad, kernel, w_in, w_out):
    local_ch, rows, width = features.shape
    size = kernel.shape[1]
    half = size // 2
    local_pos = rows * width
    count = lax.axis_size("ch")
    chips = count // 2
    me = lax.axis_index("ch")
    factor = 1.0 / math.sqrt(local_pos * lax.axis_size("sp"))

    flip = [(i, i ^ 1) for i in range(count)]
    across = lambda step: [(i, (i + 2 * step) % count) for i in range(count)]
    swap = lambda value: lax.ppermute(value, "ch", flip)
    owner = [
        lax.rem(me // 2 + step, chips) * 2 + (me % 2 if core == 0 else 1 - me % 2)
        for step in range(chips)
        for core in range(2)
    ]

    def gathered(block):
        held = []
        for step in range(chips):
            mine = block if step == 0 else lax.ppermute(block, "ch", across(chips - step))
            held += [mine, swap(mine)]
        return jnp.concatenate(held, axis=0)

    w_in_own = jnp.concatenate(
        [lax.dynamic_slice_in_dim(w_in, at * local_ch, local_ch, 0) for at in owner], axis=0
    )
    w_out_own = jnp.concatenate(
        [lax.dynamic_slice_in_dim(w_out, at * local_ch, local_ch, 1) for at in owner], axis=1
    )
    mixed_all = gathered(saved_mix.reshape(local_ch, local_pos))
    grad_all = gathered(out_grad.reshape(local_ch, local_pos))
    hidden, preact_grad = pointwise_back(mixed_all, grad_all, w_in_own, w_out_own)

    part = lambda index: matmul(
        w_in_own[index * local_ch : (index + 1) * local_ch], preact_grad
    )
    pair = [None] * chips
    for step in list(range(1, chips)) + [0]:
        away = swap(part(2 * step + 1).astype(jnp.bfloat16))
        pair[step] = part(2 * step) + away.astype(jnp.float32)
    pieces = 2 if local_ch % 32 == 0 else 1
    chunk = local_ch // pieces

    depth = up(rows + size - 1, 16)
    total = up(size * depth, 128)
    flipped = kernel[:, ::-1, ::-1].astype(jnp.float32).transpose(0, 2, 1)
    base = jnp.pad(flipped, ((0, 0), (0, 0), (0, depth - size))).reshape(local_ch, size * depth)
    base = jnp.pad(base, ((0, 0), (0, total - size * depth)))
    feat_reversed = features[:, ::-1]
    hops = lax.axis_size("sp")
    forward = [(i, i + 1) for i in range(hops - 1)]
    backward = [(i + 1, i) for i in range(hops - 1)]

    in_grads, kernel_grads = [], []
    for piece in range(pieces):
        at = slice(piece * chunk, (piece + 1) * chunk)
        mix = pair[0][at]
        for step in range(1, chips):
            sent = pair[step][at].astype(jnp.bfloat16)
            mix = mix + lax.ppermute(sent, "ch", across(step)).astype(jnp.float32)
        mix = mix.astype(jnp.bfloat16).reshape(chunk, rows, width)
        low, high, left = [], [], half
        below, above = mix, mix
        while left > 0:
            take = min(left, rows)
            below = lax.ppermute(below[:, rows - take :] if below.shape[1] >= take else below, "sp", forward)
            above = lax.ppermute(above[:, :take], "sp", backward)
            low.insert(0, below)
            high.append(above)
            left -= take
        rim = jnp.concatenate(
            low + [mix] + high + [jnp.zeros((chunk, depth - rows - size + 1, width), mix.dtype)],
            axis=1,
        )
        in_part, kernel_part = conv_back(
            rim, feat_reversed[at], out_grad[at], base[at], size
        )
        in_grads.append(in_part)
        kernel_part = kernel_part[:, : size * depth].reshape(chunk, size, depth)[:, :, :size]
        kernel_grads.append(lax.psum(kernel_part, "sp"))

    def absolute(value):
        blocks = []
        for j in range(count):
            step = lax.rem(j // 2 - me // 2 + chips, chips)
            place = step * 2 + lax.rem(me + j, 2)
            blocks.append(lax.dynamic_slice_in_dim(value, place * local_ch, local_ch, 0))
        return jnp.concatenate(blocks, axis=0)

    w_in_sum = lax.psum_scatter(
        absolute(contract_last(mixed_all, preact_grad)), "sp", scatter_dimension=1, tiled=True
    )
    w_out_sum = lax.psum_scatter(
        absolute(contract_last(grad_all, hidden)), "sp", scatter_dimension=1, tiled=True
    )
    in_grad = jnp.concatenate(in_grads, axis=0)
    kernel_grad = jnp.concatenate(kernel_grads, axis=0).transpose(0, 2, 1)[:, ::-1, ::-1] * factor
    return (in_grad, kernel_grad, w_in_sum * factor, w_out_sum.T * factor)


def solution(mesh):
    return jax.shard_map(
        per_device,
        mesh=mesh,
        in_specs=(
            P(("grp", "ch"), "sp", None),
            P(("grp", "ch"), "sp", None),
            P(("grp", "ch"), "sp", None),
            P("ch", None, None),
            P(None, "ch"),
            P("ch", None),
        ),
        out_specs=(
            P(("grp", "ch"), "sp", None),
            P(("grp", "ch"), None, None),
            P("grp", ("ch", "sp")),
            P(("grp", "ch", "sp"), None),
        ),
        check_vma=False,
    )
```

```python
import functools
import math

import jax
import jax.numpy as jnp
from jax import lax
from jax.experimental import pallas as pl
from jax.experimental.pallas import tpu as pltpu
from jax.sharding import PartitionSpec as P

SQRT_HALF = 0.7071067811865476
INV_ROOT_TAU = 0.3989422804014327
GROUP = 8


def up(count, unit):
    return -(-count // unit) * unit


def conv_kernel(size, take, low_ref, mid_ref, high_ref, feat_ref, grad_ref, base_ref, *rest):
    in_ref, part_ref = rest[-2:]
    group, rows, width = mid_ref.shape
    depth = rows + 2 * take
    half = size // 2
    total = base_ref.shape[1]
    lane = lax.broadcasted_iota(jnp.int32, (depth, width), 1)
    for c in range(group):
        rim = jnp.concatenate([low_ref[c], mid_ref[c], high_ref[c]], axis=0)
        pieces = []
        for b in range(size):
            shift = b - half
            if shift == 0:
                pieces.append(rim)
                continue
            moved = pltpu.roll(rim, (-shift) % width, 1)
            inside = (lane < width - shift) if shift > 0 else (lane >= -shift)
            pieces.append(jnp.where(inside, moved, jnp.zeros_like(moved)))
        pieces.append(jnp.zeros((total - size * depth, width), rim.dtype))
        stacked = jnp.concatenate(pieces, axis=0)
        line = jnp.broadcast_to(base_ref[c : c + 1, :], (rows, total))
        band = pltpu.roll(line, 0, 1, stride=1, stride_axis=0).astype(jnp.bfloat16)
        in_ref[c] = grad_ref[c].astype(jnp.float32) + jnp.dot(
            band, stacked, preferred_element_type=jnp.float32
        )
        cross = lax.dot_general(
            feat_ref[c], stacked, (((1,), (1,)), ((), ())), preferred_element_type=jnp.float32
        )
        aligned = pltpu.roll(cross, total - (rows - 1), 1, stride=1, stride_axis=0)
        part_ref[c : c + 1, :] = jnp.sum(aligned, axis=0, keepdims=True)


def conv_back(low, mid, high, feat_reversed, grad, base, earlier, start, size):
    channels, rows, width = mid.shape
    take = low.shape[1]
    total = base.shape[1]
    group = math.gcd(channels, GROUP)
    skip = start // group
    own = lambda *dims: pl.BlockSpec((group,) + dims, lambda i: (i,) + (0,) * len(dims))
    part = lambda *dims: pl.BlockSpec((group,) + dims, lambda i: (i + skip,) + (0,) * len(dims))
    more = [] if earlier is None else [earlier]
    return pl.pallas_call(
        functools.partial(conv_kernel, size, take),
        grid=(channels // group,),
        out_shape=(
            jax.ShapeDtypeStruct(grad.shape, jnp.float32),
            jax.ShapeDtypeStruct((channels, total), jnp.float32),
        ),
        in_specs=[own(take, width), own(rows, width), own(take, width)]
        + [part(rows, width), part(rows, width), part(total)]
        + [pl.BlockSpec(memory_space=pl.ANY) for _ in more],
        out_specs=(part(rows, width), own(total)),
        input_output_aliases={6: 0} if more else {},
        compiler_params=pltpu.CompilerParams(vmem_limit_bytes=24 * 1024 * 1024),
        cost_estimate=pl.CostEstimate(
            flops=channels * rows * width * total * 4 * 8,
            bytes_accessed=channels * width * (rows * 14) + channels * total * 8,
            transcendentals=0,
        ),
    )(low, mid, high, feat_reversed, grad, base, *more)


def contract_last(left, right):
    return lax.dot_general(
        left, right, (((1,), (1,)), ((), ())), preferred_element_type=jnp.float32
    )


def contract_first(left, right):
    return lax.dot_general(
        left, right, (((0,), (0,)), ((), ())), preferred_element_type=jnp.float32
    )


def matmul(left, right):
    return jnp.dot(left, right, preferred_element_type=jnp.float32)


def pointwise_back(mixed_rows, grad_rows, w_in_block, w_out_block):
    preact = contract_first(w_in_block, mixed_rows)
    normal_cdf = 0.5 * (1.0 + jax.scipy.special.erf(preact * SQRT_HALF))
    normal_pdf = INV_ROOT_TAU * jnp.exp(-0.5 * preact * preact)
    hidden = (preact * normal_cdf).astype(jnp.bfloat16)
    hidden_grad = matmul(w_out_block, grad_rows)
    preact_grad = (hidden_grad * (normal_cdf + preact * normal_pdf)).astype(jnp.bfloat16)
    return (hidden, preact_grad)


def per_device(features, saved_mix, out_grad, kernel, w_in, w_out):
    local_ch, rows, width = features.shape
    size = kernel.shape[1]
    half = size // 2
    local_pos = rows * width
    count = lax.axis_size("ch")
    chips = count // 2
    me = lax.axis_index("ch")
    factor = 1.0 / math.sqrt(local_pos * lax.axis_size("sp"))

    flip = [(i, i ^ 1) for i in range(count)]
    across = lambda step: [(i, (i + 2 * step) % count) for i in range(count)]
    swap = lambda value: lax.ppermute(value, "ch", flip)
    owner = [
        lax.rem(me // 2 + step, chips) * 2 + (me % 2 if core == 0 else 1 - me % 2)
        for step in range(chips)
        for core in range(2)
    ]

    def gathered(block):
        held = []
        for step in range(chips):
            mine = block if step == 0 else lax.ppermute(block, "ch", across(chips - step))
            held += [mine, swap(mine)]
        return jnp.concatenate(held, axis=0)

    w_in_own = jnp.concatenate(
        [lax.dynamic_slice_in_dim(w_in, at * local_ch, local_ch, 0) for at in owner], axis=0
    )
    w_out_own = jnp.concatenate(
        [lax.dynamic_slice_in_dim(w_out, at * local_ch, local_ch, 1) for at in owner], axis=1
    )
    hops = lax.axis_size("sp")
    depth_bits = hops.bit_length() - 1
    mine = lax.axis_index("sp")
    unit = w_in.shape[1] // hops
    order = [sum(((p >> i) & 1) << (depth_bits - 1 - i) for i in range(depth_bits)) for p in range(hops)]
    places = [jnp.bitwise_xor(mine, bits) * unit for bits in order]
    w_in_own = jnp.concatenate(
        [lax.dynamic_slice_in_dim(w_in_own, at, unit, 1) for at in places], axis=1
    )
    w_out_own = jnp.concatenate(
        [lax.dynamic_slice_in_dim(w_out_own, at, unit, 0) for at in places], axis=0
    )
    mixed_all = gathered(saved_mix.reshape(local_ch, local_pos))
    grad_all = gathered(out_grad.reshape(local_ch, local_pos))
    hidden, preact_grad = pointwise_back(mixed_all, grad_all, w_in_own, w_out_own)

    part = lambda index: matmul(
        w_in_own[index * local_ch : (index + 1) * local_ch], preact_grad
    )
    pair = [None] * chips
    for step in list(range(1, chips)) + [0]:
        away = swap(part(2 * step + 1).astype(jnp.bfloat16))
        pair[step] = part(2 * step) + away.astype(jnp.float32)
    pieces = 2 if local_ch % 32 == 0 else 1
    chunk = local_ch // pieces

    w_in_sum, w_out_sum = None, None
    span, bit = w_in.shape[1], 1
    while bit < hops:
        span //= 2
        pairs = [(i, i ^ bit) for i in range(hops)]
        trade = lambda value: lax.ppermute(value.astype(jnp.bfloat16), "sp", pairs).astype(jnp.float32)
        if bit == 1:
            w_in_away = trade(contract_last(mixed_all, preact_grad[span:]))
            w_out_away = trade(contract_last(hidden[span:], grad_all))
            w_in_sum = contract_last(mixed_all, preact_grad[:span]) + w_in_away
            w_out_sum = contract_last(hidden[:span], grad_all) + w_out_away
        else:
            w_in_sum = w_in_sum[:, :span] + trade(w_in_sum[:, span:])
            w_out_sum = w_out_sum[:span] + trade(w_out_sum[span:])
        bit *= 2

    take = min(rows, up(half, 16))
    depth = rows + 2 * take
    total = up(size * depth, 128)
    ahead = take - half
    flipped = kernel[:, ::-1, ::-1].astype(jnp.float32).transpose(0, 2, 1)
    base = jnp.pad(flipped, ((0, 0), (0, 0), (ahead, depth - size - ahead)))
    base = jnp.pad(base.reshape(local_ch, size * depth), ((0, 0), (0, total - size * depth)))
    feat_reversed = features[:, ::-1]
    forward = [(i, i + 1) for i in range(hops - 1)]
    backward = [(i + 1, i) for i in range(hops - 1)]

    def summed(lines):
        each = lines.shape[0] // hops
        shift = lambda step: [(i, (i + step) % hops) for i in range(hops)]
        cut = lambda step: lax.dynamic_slice_in_dim(lines, lax.rem(mine + step, hops) * each, each, 0)
        come = [
            lax.ppermute(cut(step).astype(jnp.bfloat16), "sp", shift(step)) for step in range(1, hops)
        ]
        block = cut(0)
        for value in come:
            block = block + value.astype(jnp.float32)
        whole = jnp.zeros_like(lines)
        for step in range(hops):
            value = block if step == 0 else lax.ppermute(block, "sp", shift(hops - step))
            whole = lax.dynamic_update_slice_in_dim(
                whole, value, lax.rem(mine + step, hops) * each, 0
            )
        return whole

    in_grad, lines = None, []
    for piece in range(pieces):
        at = slice(piece * chunk, (piece + 1) * chunk)
        mix = pair[0][at]
        for step in range(1, chips):
            sent = pair[step][at].astype(jnp.bfloat16)
            mix = mix + lax.ppermute(sent, "ch", across(step)).astype(jnp.float32)
        mix = mix.astype(jnp.bfloat16).reshape(chunk, rows, width)
        low = lax.ppermute(mix[:, rows - take :], "sp", forward)
        high = lax.ppermute(mix[:, :take], "sp", backward)
        in_grad, line = conv_back(
            low, mix, high, feat_reversed, out_grad, base, in_grad, piece * chunk, size
        )
        lines.append(summed(line))

    def absolute(value, dim):
        blocks = []
        for j in range(count):
            step = lax.rem(j // 2 - me // 2 + chips, chips)
            place = step * 2 + lax.rem(me + j, 2)
            blocks.append(lax.dynamic_slice_in_dim(value, place * local_ch, local_ch, dim))
        return jnp.concatenate(blocks, axis=dim)

    kernel_grad = [
        line[:, : size * depth]
        .reshape(-1, size, depth)[:, :, ahead : ahead + size]
        .transpose(0, 2, 1)[:, ::-1, ::-1]
        for line in lines
    ]
    kernel_grad = jnp.concatenate(kernel_grad, axis=0) * factor
    return (
        in_grad,
        kernel_grad,
        absolute(w_in_sum, 0) * factor,
        absolute(w_out_sum, 1) * factor,
    )


def solution(mesh):
    return jax.shard_map(
        per_device,
        mesh=mesh,
        in_specs=(
            P(("grp", "ch"), "sp", None),
            P(("grp", "ch"), "sp", None),
            P(("grp", "ch"), "sp", None),
            P("ch", None, None),
            P(None, "ch"),
            P("ch", None),
        ),
        out_specs=(
            P(("grp", "ch"), "sp", None),
            P(("grp", "ch"), None, None),
            P("grp", ("ch", "sp")),
            P(("grp", "ch", "sp"), None),
        ),
        check_vma=False,
    )
```

```python
import functools
import math

import jax
import jax.numpy as jnp
from jax import lax
from jax.experimental import pallas as pl
from jax.experimental.pallas import tpu as pltpu
from jax.sharding import PartitionSpec as P

SQRT_HALF = 0.7071067811865476
INV_ROOT_TAU = 0.3989422804014327
GROUP = 8


def up(count, unit):
    return -(-count // unit) * unit


def conv_kernel(size, take, low_ref, mid_ref, high_ref, feat_ref, grad_ref, base_ref, *rest):
    in_ref, part_ref = rest[-2:]
    group, rows, width = mid_ref.shape
    depth = rows + 2 * take
    half = size // 2
    total = base_ref.shape[1]
    lane = lax.broadcasted_iota(jnp.int32, (depth, width), 1)
    for c in range(group):
        rim = jnp.concatenate([low_ref[c], mid_ref[c], high_ref[c]], axis=0)
        pieces = []
        for b in range(size):
            shift = b - half
            if shift == 0:
                pieces.append(rim)
                continue
            moved = pltpu.roll(rim, (-shift) % width, 1)
            inside = (lane < width - shift) if shift > 0 else (lane >= -shift)
            pieces.append(jnp.where(inside, moved, jnp.zeros_like(moved)))
        pieces.append(jnp.zeros((total - size * depth, width), rim.dtype))
        stacked = jnp.concatenate(pieces, axis=0)
        line = jnp.broadcast_to(base_ref[c : c + 1, :], (rows, total))
        band = pltpu.roll(line, 0, 1, stride=1, stride_axis=0).astype(jnp.bfloat16)
        in_ref[c] = grad_ref[c].astype(jnp.float32) + jnp.dot(
            band, stacked, preferred_element_type=jnp.float32
        )
        cross = lax.dot_general(
            feat_ref[c], stacked, (((1,), (1,)), ((), ())), preferred_element_type=jnp.float32
        )
        aligned = pltpu.roll(cross, total - (rows - 1), 1, stride=1, stride_axis=0)
        part_ref[c : c + 1, :] = jnp.sum(aligned, axis=0, keepdims=True)


def conv_back(low, mid, high, feat_reversed, grad, base, earlier, first, start, channels, size):
    rows, width = mid.shape[1:]
    take = low.shape[1]
    total = base.shape[1]
    group = math.gcd(channels, GROUP)
    skip, near = start // group, (start - first) // group
    own = lambda *dims: pl.BlockSpec((group,) + dims, lambda i: (i,) + (0,) * len(dims))
    rim = lambda *dims: pl.BlockSpec((group,) + dims, lambda i: (i + near,) + (0,) * len(dims))
    part = lambda *dims: pl.BlockSpec((group,) + dims, lambda i: (i + skip,) + (0,) * len(dims))
    more = [] if earlier is None else [earlier]
    return pl.pallas_call(
        functools.partial(conv_kernel, size, take),
        grid=(channels // group,),
        out_shape=(
            jax.ShapeDtypeStruct(grad.shape, jnp.float32),
            jax.ShapeDtypeStruct((channels, total), jnp.float32),
        ),
        in_specs=[rim(take, width), rim(rows, width), rim(take, width)]
        + [part(rows, width), part(rows, width), part(total)]
        + [pl.BlockSpec(memory_space=pl.ANY) for _ in more],
        out_specs=(part(rows, width), own(total)),
        input_output_aliases={6: 0} if more else {},
        compiler_params=pltpu.CompilerParams(vmem_limit_bytes=24 * 1024 * 1024),
        cost_estimate=pl.CostEstimate(
            flops=channels * rows * width * total * 4 * 8,
            bytes_accessed=channels * width * (rows * 14) + channels * total * 8,
            transcendentals=0,
        ),
    )(low, mid, high, feat_reversed, grad, base, *more)


def contract_last(left, right):
    return lax.dot_general(
        left, right, (((1,), (1,)), ((), ())), preferred_element_type=jnp.float32
    )


def contract_first(left, right):
    return lax.dot_general(
        left, right, (((0,), (0,)), ((), ())), preferred_element_type=jnp.float32
    )


def matmul(left, right):
    return jnp.dot(left, right, preferred_element_type=jnp.float32)


def pointwise_back(mixed_rows, grad_rows, w_in_block, w_out_block):
    preact = contract_first(w_in_block, mixed_rows)
    normal_cdf = 0.5 * (1.0 + jax.scipy.special.erf(preact * SQRT_HALF))
    normal_pdf = INV_ROOT_TAU * jnp.exp(-0.5 * preact * preact)
    hidden = (preact * normal_cdf).astype(jnp.bfloat16)
    hidden_grad = matmul(w_out_block, grad_rows)
    preact_grad = (hidden_grad * (normal_cdf + preact * normal_pdf)).astype(jnp.bfloat16)
    return (hidden, preact_grad)


def per_device(features, saved_mix, out_grad, kernel, w_in, w_out):
    local_ch, rows, width = features.shape
    size = kernel.shape[1]
    half = size // 2
    local_pos = rows * width
    count = lax.axis_size("ch")
    chips = count // 2
    me = lax.axis_index("ch")
    factor = 1.0 / math.sqrt(local_pos * lax.axis_size("sp"))

    flip = [(i, i ^ 1) for i in range(count)]
    across = lambda step: [(i, (i + 2 * step) % count) for i in range(count)]
    swap = lambda value: lax.ppermute(value, "ch", flip)
    owner = [
        lax.rem(me // 2 + step, chips) * 2 + (me % 2 if core == 0 else 1 - me % 2)
        for step in range(chips)
        for core in range(2)
    ]

    def gathered(block):
        held = []
        for step in range(chips):
            mine = block if step == 0 else lax.ppermute(block, "ch", across(chips - step))
            held += [mine, swap(mine)]
        return jnp.concatenate(held, axis=0)

    w_in_own = jnp.concatenate(
        [lax.dynamic_slice_in_dim(w_in, at * local_ch, local_ch, 0) for at in owner], axis=0
    )
    w_out_own = jnp.concatenate(
        [lax.dynamic_slice_in_dim(w_out, at * local_ch, local_ch, 1) for at in owner], axis=1
    )
    hops = lax.axis_size("sp")
    depth_bits = hops.bit_length() - 1
    mine = lax.axis_index("sp")
    unit = w_in.shape[1] // hops
    order = [sum(((p >> i) & 1) << (depth_bits - 1 - i) for i in range(depth_bits)) for p in range(hops)]
    places = [jnp.bitwise_xor(mine, bits) * unit for bits in order]
    w_in_own = jnp.concatenate(
        [lax.dynamic_slice_in_dim(w_in_own, at, unit, 1) for at in places], axis=1
    )
    w_out_own = jnp.concatenate(
        [lax.dynamic_slice_in_dim(w_out_own, at, unit, 0) for at in places], axis=0
    )
    mixed_all = gathered(saved_mix.reshape(local_ch, local_pos))
    grad_all = gathered(out_grad.reshape(local_ch, local_pos))
    hidden, preact_grad = pointwise_back(mixed_all, grad_all, w_in_own, w_out_own)

    part = lambda index: matmul(
        w_in_own[index * local_ch : (index + 1) * local_ch], preact_grad
    )
    pair = [None] * chips
    for step in list(range(1, chips)) + [0]:
        away = swap(part(2 * step + 1).astype(jnp.bfloat16))
        pair[step] = part(2 * step) + away.astype(jnp.float32)
    chunk = local_ch // 2

    take = min(rows, up(half, 16))
    depth = rows + 2 * take
    total = up(size * depth, 128)
    ahead = take - half
    flipped = kernel[:, ::-1, ::-1].astype(jnp.float32).transpose(0, 2, 1)
    base = jnp.pad(flipped, ((0, 0), (0, 0), (ahead, depth - size - ahead)))
    base = jnp.pad(base.reshape(local_ch, size * depth), ((0, 0), (0, total - size * depth)))
    feat_reversed = features[:, ::-1]
    forward = [(i, i + 1) for i in range(hops - 1)]
    backward = [(i + 1, i) for i in range(hops - 1)]

    shift = lambda step: [(i, (i + step) % hops) for i in range(hops)]

    def scattered(lines):
        each = lines.shape[0] // hops
        cut = lambda step: lax.dynamic_slice_in_dim(lines, lax.rem(mine + step, hops) * each, each, 0)
        return [cut(0)] + [
            lax.ppermute(cut(step).astype(jnp.bfloat16), "sp", shift(step)) for step in range(1, hops)
        ]

    def added(blocks):
        return sum((value.astype(jnp.float32) for value in blocks[1:]), blocks[0])

    def spread(block):
        return [block] + [lax.ppermute(block, "sp", shift(hops - step)) for step in range(1, hops)]

    def placed(blocks):
        each, total = blocks[0].shape
        whole = jnp.zeros((each * hops, total), jnp.float32)
        for step, value in enumerate(blocks):
            whole = lax.dynamic_update_slice_in_dim(whole, value, lax.rem(mine + step, hops) * each, 0)
        return whole

    tie = lambda value, *others: lax.optimization_barrier((value,) + others)[0]
    narrow = lambda value: value.astype(jnp.bfloat16)
    wide = lambda value: value.astype(jnp.float32)

    def arrived(piece):
        at = slice(piece * chunk, (piece + 1) * chunk)
        come = [
            lax.ppermute(narrow(pair[step][at]), "ch", across(step)) for step in range(1, chips)
        ]
        return pair[0][at], come

    def mixed(mine, come):
        for value in come:
            mine = mine + wide(value)
        return narrow(mine).reshape(chunk, rows, width)

    def rimmed(mix):
        return (
            lax.ppermute(mix[:, rows - take :], "sp", forward),
            mix,
            lax.ppermute(mix[:, :take], "sp", backward),
        )

    def traded(values, bit):
        pairs = [(i, i ^ bit) for i in range(hops)]
        return [lax.ppermute(value, "sp", pairs) for value in values]

    span = w_in.shape[1] // 2
    part_ch = chunk // 2

    def conv(rim, earlier, index):
        return conv_back(
            *rim, feat_reversed, out_grad, base, earlier, index // 2 * chunk, index * part_ch, part_ch, size
        )

    mine_a, come_a = arrived(0)
    mine_b, come_b = arrived(1)
    mix_a = mixed(mine_a, come_a)
    rim_a = rimmed(mix_a)
    late_grad, late_hidden = lax.optimization_barrier((preact_grad, hidden, mix_a))[:2]
    sent = (
        narrow(contract_last(mixed_all, late_grad[span:])),
        narrow(contract_last(late_hidden[span:], grad_all)),
    )
    w_in_sum = contract_last(mixed_all, late_grad[:span])
    w_out_sum = contract_last(late_hidden[:span], grad_all)
    away = traded(sent, 1)
    w_in_sum, w_out_sum, low = lax.optimization_barrier((w_in_sum, w_out_sum, rim_a[0], *sent))[:3]
    rim_a = (low,) + rim_a[1:]
    in_grad, line0 = conv(rim_a, None, 0)
    come_b = [tie(value, line0) for value in come_b]
    mix_b = mixed(mine_b, come_b)
    rim_b = rimmed(mix_b)
    in_grad, line1 = conv((tie(rim_a[0], mix_b), rim_a[1], rim_a[2]), in_grad, 1)
    away = [tie(value, line1) for value in away]
    w_in_sum = w_in_sum + wide(away[0])
    w_out_sum = w_out_sum + wide(away[1])
    w_sums, bit, sent = (w_in_sum, w_out_sum), 2, ()

    def halves(sums, span):
        return (narrow(sums[0][:, span:]), narrow(sums[1][span:]))

    if bit < hops:
        span //= 2
        sent = halves(w_sums, span)
        away = traded(sent, bit)
    blocks_a = scattered(jnp.concatenate([line0, line1], axis=0))
    in_grad, line2 = conv((tie(rim_b[0], *sent), rim_b[1], rim_b[2]), in_grad, 2)
    if bit < hops:
        away = [tie(value, line2) for value in away]
    while bit < hops:
        w_sums = (w_sums[0][:, :span] + wide(away[0]), w_sums[1][:span] + wide(away[1]))
        bit *= 2
        if bit < hops:
            span //= 2
            away = traded(halves(w_sums, span), bit)
    w_in_sum, w_out_sum = w_sums
    block_a = added([blocks_a[0]] + [tie(value, line2) for value in blocks_a[1:]])
    whole_a = spread(block_a)
    in_grad, line3 = conv((tie(rim_b[0], block_a), rim_b[1], rim_b[2]), in_grad, 3)
    line3 = lax.optimization_barrier((line3, *whole_a[1:]))
    whole_a = [whole_a[0], *line3[1:]]
    blocks_b = scattered(jnp.concatenate([line2, line3[0]], axis=0))
    lines = [placed(whole_a), placed(spread(added(blocks_b)))]

    def absolute(value, dim):
        blocks = []
        for j in range(count):
            step = lax.rem(j // 2 - me // 2 + chips, chips)
            place = step * 2 + lax.rem(me + j, 2)
            blocks.append(lax.dynamic_slice_in_dim(value, place * local_ch, local_ch, dim))
        return jnp.concatenate(blocks, axis=dim)

    kernel_grad = [
        line[:, : size * depth]
        .reshape(-1, size, depth)[:, :, ahead : ahead + size]
        .transpose(0, 2, 1)[:, ::-1, ::-1]
        for line in lines
    ]
    kernel_grad = jnp.concatenate(kernel_grad, axis=0) * factor
    return (
        in_grad,
        kernel_grad,
        absolute(w_in_sum, 0) * factor,
        absolute(w_out_sum, 1) * factor,
    )


def solution(mesh):
    return jax.shard_map(
        per_device,
        mesh=mesh,
        in_specs=(
            P(("grp", "ch"), "sp", None),
            P(("grp", "ch"), "sp", None),
            P(("grp", "ch"), "sp", None),
            P("ch", None, None),
            P(None, "ch"),
            P("ch", None),
        ),
        out_specs=(
            P(("grp", "ch"), "sp", None),
            P(("grp", "ch"), None, None),
            P("grp", ("ch", "sp")),
            P(("grp", "ch", "sp"), None),
        ),
        check_vma=False,
    )
```
